32 devices in a mesh: dp: 8 (over z, x), fsdp: 4 (over y, core).
Axes of the slice: x: 2, y: 2, z: 4, core: 2. Of those that a mesh axis runs over, the one named last changes fastest.
Arguments:
- frames: bfloat16 [128, 128, 1024], P(('dp', 'fsdp')), may hold values from -6 to 6
- frame_mask: int32 [128, 128], P(('dp', 'fsdp')), may hold values 0 or 1
- motion_weight: bfloat16 [1024, 512], replicated, may hold values from -0.1875 to 0.1875
- caption_feats: bfloat16 [2048, 4096], P(('dp', 'fsdp')), may hold values from -6 to 6
- text_weight: bfloat16 [4096, 512], P('fsdp'), may hold values from -0.09375 to 0.09375
- caption_route: int32 [2048, 1], P(('dp', 'fsdp')), may hold values from 0 to 7; in each aligned block of 64 rows (0 to 63, 64 to 127, ...) at most 16 rows name the same one
- caption_clip: int32 [2048], P(('dp', 'fsdp')), may hold values from 0 to 15
Outputs:
- clip_loss: float32 [128], P(('dp', 'fsdp'))
- motion_grad: float32 [128, 512], P(('dp', 'fsdp'))
The draws below stay inside these ranges and needn't reach their ends.
Inputs may be any that keep to these rules, and one draw needn't show every extreme that they name: `caption_route`: no group is named by more than 16 of one device's captions; in some devices' captions one group is named exactly 16 times.
All inputs are finite; a program needn't handle non-finite values. No bound on the sum of `frame_mask` on one device may be relied on, other than what follows from the above.
Results may differ from the reference program's by a relative error of at most 0.0037.
Values may be sent and summed in bfloat16 or wider, within the bound.
A program may use at most 64 MiB of HBM per device.

```python
import math
import jax
import jax.numpy as jnp
import numpy as np
from jax import lax

D = 1024
EMB = 512
TEXT = 4096
FRAMES = 128
CLIP_DEV = 4
CAP_DEV = 64
SLOTS = 16
CLIPS = 128
CAPTIONS = 2048
GRP_CLIPS = 16
CAP_GRP = 256
N_DP = 8


def set_ends(entries, rng, smallest, largest):
    dims = entries.shape
    index_at = [jax.random.randint(jax.random.fold_in(rng, axis), (), 0, dims[axis]) for axis in range(len(dims))]
    entries = entries.at[tuple(index_at)].set(smallest)
    longest = dims.index(max(dims))
    index_at[longest] = (index_at[longest] + 1) % dims[longest]
    return entries.at[tuple(index_at)].set(largest)


def shard_levels(stream_key, shape, split, smallest, top_value):
    def one(position, blocks):
        draws = jax.random.uniform(jax.random.fold_in(jax.random.fold_in(stream_key, 6), position), (blocks,), jnp.float32, smallest / len(split), top_value / len(split))
        return jnp.repeat(jnp.exp(draws), shape[position] // blocks).reshape((-1,) + (1,) * (len(shape) - position - 1))

    gain = one(*split[0])
    for cut in split[1:]:
        gain = gain * one(*cut)
    return gain


def assign_block(key, own, number, rows, count, top, most, slope):
    ranking = jax.random.permutation(key, count)
    packed, ordinary = shares(count, rows * top, most, slope, True), shares(count, rows * top, most, slope, False)
    places = jnp.arange(count)

    def named(lengths, rotation):
        used = int((lengths > 0).sum())
        fixed = max(1, used // 4)
        passed = fixed + (places - fixed + rotation * (used - fixed)) % max(1, count - fixed)
        return jnp.zeros((count,), jnp.int32).at[ranking[jnp.where(places < fixed, places, passed)]].set(jnp.asarray(lengths, jnp.int32))

    lengths = jnp.where(number % 4 == 0, named(packed, number // 4), named(ordinary, number - number // 4 - 1))
    mixed = jax.random.permutation(jax.random.fold_in(own, 3), count)
    source_of, taker = mixed[0:count // 2 * 2:2], mixed[1:count // 2 * 2:2]
    margin = jnp.minimum(lengths[source_of] - 1, most - lengths[taker]) // 2
    margin = jnp.where((source_of == ranking[0]) | (taker == ranking[0]) | (lengths[taker] == 0), 0, jnp.maximum(margin, 0))
    passed = jax.random.randint(jax.random.fold_in(own, 4), (count // 2,), 0, 1 << 20) % (margin + 1)
    lengths = lengths.at[source_of].add(-passed).at[taker].add(passed)
    labels = jnp.searchsorted(jnp.cumsum(lengths), jnp.arange(rows * top), side="right").astype(jnp.int32)
    grid = labels.reshape(top, rows).T
    grid = grid[jax.random.permutation(jax.random.fold_in(own, 1), rows)]
    rotation = jax.random.randint(jax.random.fold_in(own, 2), (rows, 1), 0, top)
    return jnp.take_along_axis(grid, (jnp.arange(top)[None, :] + rotation) % top, axis=1)


def shares(count, total, bound, skew, full):
    loads = [(1 << 20) // math.isqrt(standing ** skew) + 1 for standing in range(1, count + 1)]
    largest = bound if full else min(bound, max(-(-total // count), total * loads[0] // sum(loads)))
    least = 1 if total - largest >= count - 1 else 0
    counts, rest = [largest] + [least] * (count - 1), total - largest - least * (count - 1)
    while rest > 0:
        movable = [i for i in range(1, count) if counts[i] < largest] or [i for i in range(1, count) if counts[i] < bound]
        whole, left = sum([loads[i] for i in movable]), rest
        for i in movable:
            more = min(bound - counts[i], max(1, left * loads[i] // whole), rest)
            counts[i] = counts[i] + more
            rest = rest - more
    return np.array(counts)


def scatter_about(key, extent, deviation, most, cuts=(), kind=jnp.bfloat16):
    result = deviation * jax.random.normal(key, extent, jnp.float32)
    if cuts:
        result = result * shard_levels(key, extent, cuts, -0.22, 0.18)
    return jnp.clip(result, -most, most).astype(kind)


def setup_inputs(seed: int = 0) -> dict:
    streams_of = jax.random.split(jax.random.key(seed), 8)
    frames = scatter_about(streams_of[0], (CLIPS, FRAMES, D), 1.0, 6.0, ((0, 32),))
    frame_mask = set_ends((jax.random.randint(streams_of[1], (CLIPS, FRAMES), 0, 4) < 3).astype(jnp.int32), jax.random.fold_in(streams_of[1], 1), 0, 1)
    motion_weight = scatter_about(streams_of[2], (D, EMB), D ** -0.5, 0.1875)
    caption_feats = scatter_about(streams_of[3], (CAPTIONS, TEXT), 1.0, 6.0, ((0, 32),))
    text_weight = scatter_about(streams_of[4], (TEXT, EMB), TEXT ** -0.5, 0.09375, ((0, 4),))
    caption_route_keys = jax.random.split(jax.random.fold_in(streams_of[5], 1), CAPTIONS // CAP_DEV)
    caption_route_turns = jax.random.permutation(jax.random.fold_in(streams_of[5], 3), CAPTIONS // CAP_DEV)
    caption_route = jax.vmap(lambda own, number: assign_block(jax.random.fold_in(streams_of[5], 2), own, number, CAP_DEV, N_DP, 1, SLOTS, 2))(caption_route_keys, caption_route_turns).reshape((CAPTIONS, 1))
    caption_clip = set_ends(jax.random.randint(streams_of[6], (CAPTIONS,), 0, GRP_CLIPS), jax.random.fold_in(streams_of[6], 1), 0, GRP_CLIPS - 1).astype(jnp.int32)
    return {"frames": frames, "frame_mask": frame_mask, "motion_weight": motion_weight, "caption_feats": caption_feats, "text_weight": text_weight, "caption_route": caption_route, "caption_clip": caption_clip}


def normalize(values):
    return (values * lax.rsqrt(lax.optimization_barrier(jnp.sum(values * values, axis=-1, keepdims=True)) + 1e-06)).astype(jnp.bfloat16)

def reference(frames, frame_mask, motion_weight, caption_feats, text_weight, caption_route, caption_clip):

    def encode(index):
        block = lax.dynamic_slice_in_dim(frames, index * GRP_CLIPS, GRP_CLIPS, 0)
        keep = lax.dynamic_slice_in_dim(frame_mask, index * GRP_CLIPS, GRP_CLIPS, 0).astype(jnp.float32)
        hidden = jax.nn.gelu(jnp.dot(block.reshape(-1, D), motion_weight, preferred_element_type=jnp.float32))
        hidden = hidden.reshape(GRP_CLIPS, FRAMES, EMB)
        return normalize(lax.optimization_barrier(jnp.sum(hidden * keep[:, :, None], axis=1)))
    motion_emb = lax.map(encode, jnp.arange(N_DP, dtype=jnp.int32))

    def step(carry, index):
        grad_acc, loss_acc = carry
        feats = lax.dynamic_slice_in_dim(caption_feats, index * CAP_GRP, CAP_GRP, 0)
        target = lax.dynamic_slice_in_dim(caption_route, index * CAP_GRP, CAP_GRP, 0)[:, 0]
        clip_ids = lax.dynamic_slice_in_dim(caption_clip, index * CAP_GRP, CAP_GRP, 0)
        text_emb = normalize(jnp.dot(feats, text_weight, preferred_element_type=jnp.float32))
        chosen = motion_emb[target]
        scores = jnp.einsum('ce,cme->cm', text_emb.astype(jnp.float32), chosen.astype(jnp.float32)) / 0.07
        lse_vals = jnp.log(lax.optimization_barrier(jnp.sum(jnp.exp(scores), axis=1)))
        onehot = (clip_ids[:, None] == jnp.arange(GRP_CLIPS, dtype=jnp.int32)[None, :]).astype(jnp.float32)
        losses = lse_vals - lax.optimization_barrier(jnp.sum(onehot * scores, axis=1))
        coefficient = (jnp.exp(scores - lse_vals[:, None]) - onehot).astype(jnp.bfloat16)
        outer = coefficient.astype(jnp.float32)[:, :, None] * text_emb.astype(jnp.float32)[:, None, :]
        grad_acc = grad_acc + jax.ops.segment_sum(outer, target, num_segments=N_DP)
        loss_acc = loss_acc + jax.ops.segment_sum(onehot * losses[:, None], target, num_segments=N_DP)
        return ((grad_acc, loss_acc), None)
    start_state = (jnp.zeros((N_DP, GRP_CLIPS, EMB), jnp.float32), jnp.zeros((N_DP, GRP_CLIPS), jnp.float32))
    (grad_acc, loss_acc), _ = lax.scan(step, start_state, jnp.arange(N_DP, dtype=jnp.int32))
    clip_loss = loss_acc.reshape(CLIPS) * (CLIP_DEV / CAP_DEV)
    motion_grad = grad_acc.reshape(CLIPS, EMB) / 0.07
    return (clip_loss, motion_grad)
```

```python
import functools

import jax
import jax.numpy as jnp
from jax import lax
from jax.experimental import pallas as pl
from jax.experimental.pallas import tpu as pltpu
from jax.sharding import PartitionSpec as P

HALVES = 2
LOSS_LANES = 128
F32 = jnp.float32
BF16 = jnp.bfloat16


def normalize(values):
    return values * lax.rsqrt(jnp.sum(values * values, axis=-1, keepdims=True) + 1e-06)


def gelu(x):
    return 0.5 * x * (1.0 + jnp.tanh(0.7978845608028654 * (x + 0.044715 * (x * x * x))))


def remote(src, dst, send, recv, axis, index):
    return pltpu.make_async_remote_copy(
        src_ref=src,
        dst_ref=dst,
        send_sem=send,
        recv_sem=recv,
        device_id={axis: index},
        device_id_type=pl.DeviceIdType.MESH,
    )


def kernel(
    groups,
    shards,
    frames_hbm,
    weight_hbm,
    caps_hbm,
    text_hbm,
    mask_ref,
    route_ref,
    clip_ref,
    grad_out,
    loss_out,
    frames_v,
    weight_v,
    own_caps,
    text_v,
    cap_recv,
    part_send,
    part_recv,
    clip_slots,
    grp_rows,
    all_motion,
    grad_send,
    grad_recv,
    sum_slots,
    sum_recv,
    local_sem,
    cap_ss,
    cap_rs,
    part_ss,
    part_rs,
    m1_ss,
    m1_rs,
    m2_ss,
    m2_rs,
    g1_ss,
    g1_rs,
    g2_ss,
    g2_rs,
):
    me_g, me_f = lax.axis_index("dp"), lax.axis_index("fsdp")
    clip_dev, frame_count, _ = frames_v.shape
    cap_dev, depth = own_caps.shape
    emb = text_v.shape[1]
    rows = cap_dev // HALVES
    block = groups * clip_dev
    clips = block * shards

    def shard(k):
        return lax.rem(me_f + (k + shards), shards)

    def group(k):
        return lax.rem(me_g + (k + groups), groups)

    def columns(owner):
        return pl.ds(pl.multiple_of(owner * depth, depth), depth)

    loads = [
        pltpu.make_async_copy(frames_hbm, frames_v, local_sem.at[0]),
        pltpu.make_async_copy(weight_hbm, weight_v, local_sem.at[1]),
        pltpu.make_async_copy(text_hbm, text_v, local_sem.at[2]),
        pltpu.make_async_copy(caps_hbm.at[:, columns(me_f)], own_caps, local_sem.at[3]),
    ]
    for load in loads:
        load.start()

    barrier = pltpu.get_barrier_semaphore()
    for k in range(1, shards):
        pl.semaphore_signal(
            barrier, inc=1, device_id={"fsdp": shard(k)}, device_id_type=pl.DeviceIdType.MESH
        )
    for k in range(1, groups):
        pl.semaphore_signal(
            barrier, inc=1, device_id={"dp": group(k)}, device_id_type=pl.DeviceIdType.MESH
        )
    pl.semaphore_wait(barrier, shards + groups - 2)

    offsets = sorted(range(1, shards), key=lambda k: abs(k - shards // 2))
    cap_copies = {}
    for h in range(HALVES):
        for k in offsets:
            cap_copies[h, k] = remote(
                caps_hbm.at[pl.ds(h * rows, rows), columns(shard(k))],
                cap_recv.at[h, k - 1],
                cap_ss.at[h, k - 1],
                cap_rs.at[h, k - 1],
                "fsdp",
                shard(k),
            )
            cap_copies[h, k].start()

    loads[0].wait()
    loads[1].wait()
    eye = (
        lax.broadcasted_iota(jnp.int32, (frame_count, frame_count), 0)
        == lax.broadcasted_iota(jnp.int32, (frame_count, frame_count), 1)
    ).astype(F32)
    for clip in range(clip_dev):
        hidden = gelu(jnp.dot(frames_v[clip], weight_v[...], preferred_element_type=F32))
        keep = jnp.sum(eye * mask_ref[pl.ds(clip, 1), :].astype(F32), axis=1, keepdims=True)
        pooled = jnp.sum(hidden * keep, axis=0, keepdims=True)
        clip_slots[me_f, pl.ds(clip, 1), :] = normalize(pooled).astype(BF16).astype(F32)
    m1 = []
    for k in range(1, shards):
        copy = remote(
            clip_slots.at[me_f],
            clip_slots.at[me_f],
            m1_ss.at[k - 1],
            m1_rs.at[k - 1],
            "fsdp",
            shard(k),
        )
        copy.start()
        m1.append(copy)

    loads[2].wait()
    loads[3].wait()
    text_raw = jnp.dot(own_caps[...], text_v[...], preferred_element_type=F32)
    part_copies = []

    def project(h):
        for k in offsets:
            cap_copies[h, k].wait_recv()
        arrived = cap_recv[h].reshape((shards - 1) * rows, depth)
        partial = jnp.dot(arrived, text_v[...], preferred_element_type=F32).astype(BF16)
        for k in offsets:
            part_send[h, k - 1] = partial[(k - 1) * rows : k * rows, :]
            copy = remote(
                part_send.at[h, k - 1],
                part_recv.at[k - 1, pl.ds(h * rows, rows)],
                part_ss.at[h, k - 1],
                part_rs.at[h, k - 1],
                "fsdp",
                shard(-k),
            )
            copy.start()
            part_copies.append(copy)

    project(0)

    for k in range(1, shards):
        remote(
            clip_slots.at[me_f],
            clip_slots.at[shard(-k)],
            m1_ss.at[k - 1],
            m1_rs.at[k - 1],
            "fsdp",
            shard(-k),
        ).wait_recv()
    for f in range(shards):
        grp_rows[pl.ds(f * clip_dev, clip_dev), :] = clip_slots[f]
    all_motion[me_g] = grp_rows[...].astype(BF16)
    m2 = []
    for k in range(1, groups):
        copy = remote(
            all_motion.at[me_g],
            all_motion.at[me_g],
            m2_ss.at[k - 1],
            m2_rs.at[k - 1],
            "dp",
            group(k),
        )
        copy.start()
        m2.append(copy)

    for h in range(1, HALVES):
        project(h)

    for k in range(1, groups):
        remote(
            all_motion.at[me_g],
            all_motion.at[group(-k)],
            m2_ss.at[k - 1],
            m2_rs.at[k - 1],
            "dp",
            group(-k),
        ).wait_recv()
    gathered = all_motion[...].reshape(clips, emb)
    pieces = []
    for f in range(shards):
        r = lax.broadcasted_iota(jnp.int32, (block, clips), 0)
        c = lax.broadcasted_iota(jnp.int32, (block, clips), 1)
        want = (r // clip_dev) * (clip_dev * shards) + f * clip_dev + (r & (clip_dev - 1))
        pick = (c == want).astype(F32).astype(BF16)
        pieces.append(jnp.dot(pick, gathered, preferred_element_type=F32).astype(BF16))
    motion = jnp.concatenate(pieces, axis=0)

    route, chosen = route_ref[...], clip_ref[...]
    r = lax.broadcasted_iota(jnp.int32, (clips, cap_dev), 0)
    in_group = ((r & (block - 1)) // clip_dev) == route
    target = in_group & (((r // block) * clip_dev + (r & (clip_dev - 1))) == chosen)

    for copy in part_copies:
        copy.wait_recv()
    for k in range(1, shards):
        text_raw = text_raw + part_recv[k - 1].astype(F32)
    text_emb = normalize(text_raw).astype(BF16)

    scores = (
        lax.dot_general(motion, text_emb, (((1,), (1,)), ((), ())), preferred_element_type=F32)
        / 0.07
    )
    power = jnp.where(in_group, jnp.exp(scores), 0.0)
    total = jnp.sum(power, axis=0, keepdims=True)
    lse = jnp.log(total)
    onehot = target.astype(F32)
    losses = lse - jnp.sum(onehot * scores, axis=0, keepdims=True)
    coefficient = (power * (1.0 / total) - onehot).astype(BF16)
    grad = jnp.dot(coefficient, text_emb, preferred_element_type=F32)
    loss_term = jnp.sum(onehot * losses, axis=1, keepdims=True)
    high = loss_term.astype(BF16).astype(F32)
    lane = lax.broadcasted_iota(jnp.int32, (clips, LOSS_LANES), 1)
    loss_pair = jnp.where(lane < LOSS_LANES // 2, high, loss_term - high).astype(BF16)
    grad = grad.astype(BF16)
    g1 = []
    for f in range(shards):
        grad_send[f, :, pl.ds(0, emb)] = grad[f * block : (f + 1) * block, :]
        grad_send[f, :, pl.ds(emb, LOSS_LANES)] = loss_pair[f * block : (f + 1) * block, :]
    for k in offsets:
        copy = remote(
            grad_send.at[shard(k)],
            grad_recv.at[k - 1],
            g1_ss.at[k - 1],
            g1_rs.at[k - 1],
            "fsdp",
            shard(k),
        )
        copy.start()
        g1.append(copy)
    summed = grad_send[me_f].astype(F32)
    for copy in g1:
        copy.wait_recv()
    for k in range(1, shards):
        summed = summed + grad_recv[k - 1].astype(F32)
    for g in range(groups):
        sum_slots[g] = summed[g * clip_dev : (g + 1) * clip_dev, :]
    g2 = []
    for k in range(1, groups):
        copy = remote(
            sum_slots.at[group(k)],
            sum_recv.at[k - 1],
            g2_ss.at[k - 1],
            g2_rs.at[k - 1],
            "dp",
            group(k),
        )
        copy.start()
        g2.append(copy)
    final = sum_slots[me_g]
    for copy in g2:
        copy.wait_recv()
    for k in range(1, groups):
        final = final + sum_recv[k - 1]
    grad_out[...] = final[:, :emb] / 0.07
    loss = final[:, emb : emb + 1] + final[:, emb + LOSS_LANES // 2 : emb + LOSS_LANES // 2 + 1]
    corner = lax.broadcasted_iota(
        jnp.int32, (clip_dev, clip_dev), 0
    ) == lax.broadcasted_iota(jnp.int32, (clip_dev, clip_dev), 1)
    loss_out[...] = jnp.sum(jnp.where(corner, loss, 0.0), axis=0, keepdims=True) * (
        clip_dev / cap_dev
    )

    for copy in [*cap_copies.values(), *part_copies, *m1, *m2, *g1, *g2]:
        copy.wait_send()


def local(
    frames, frame_mask, motion_weight, caption_feats, text_weight, caption_route, caption_clip
):
    groups, shards = lax.axis_size("dp"), lax.axis_size("fsdp")
    clip_dev = frames.shape[0]
    cap_dev = caption_feats.shape[0]
    depth, emb = text_weight.shape
    rows = cap_dev // HALVES
    block = groups * clip_dev
    wide = emb + LOSS_LANES
    hbm, vmem = pl.BlockSpec(memory_space=pl.ANY), pl.BlockSpec(memory_space=pltpu.VMEM)
    dma = pltpu.SemaphoreType.DMA
    grad, loss = pl.pallas_call(
        functools.partial(kernel, groups, shards),
        out_shape=(
            jax.ShapeDtypeStruct((clip_dev, emb), F32),
            jax.ShapeDtypeStruct((1, clip_dev), F32),
        ),
        in_specs=[hbm] * 4 + [vmem] * 3,
        out_specs=(vmem, vmem),
        scratch_shapes=[
            pltpu.VMEM(frames.shape, BF16),
            pltpu.VMEM(motion_weight.shape, BF16),
            pltpu.VMEM((cap_dev, depth), BF16),
            pltpu.VMEM((depth, emb), BF16),
            pltpu.VMEM((HALVES, shards - 1, rows, depth), BF16),
            pltpu.VMEM((HALVES, shards - 1, rows, emb), BF16),
            pltpu.VMEM((shards - 1, cap_dev, emb), BF16),
            pltpu.VMEM((shards, clip_dev, emb), F32),
            pltpu.VMEM((shards * clip_dev, emb), F32),
            pltpu.VMEM((groups, shards * clip_dev, emb), BF16),
            pltpu.VMEM((shards, block, wide), BF16),
            pltpu.VMEM((shards - 1, block, wide), BF16),
            pltpu.VMEM((groups, clip_dev, wide), F32),
            pltpu.VMEM((groups - 1, clip_dev, wide), F32),
            dma((4,)),
            dma((HALVES, shards - 1)),
            dma((HALVES, shards - 1)),
            dma((HALVES, shards - 1)),
            dma((HALVES, shards - 1)),
            dma((shards - 1,)),
            dma((shards - 1,)),
            dma((groups - 1,)),
            dma((groups - 1,)),
            dma((shards - 1,)),
            dma((shards - 1,)),
            dma((groups - 1,)),
            dma((groups - 1,)),
        ],
        compiler_params=pltpu.CompilerParams(
            collective_id=0, has_side_effects=True, vmem_limit_bytes=56 * 1024 * 1024
        ),
    )(
        frames,
        motion_weight,
        caption_feats,
        text_weight,
        frame_mask,
        caption_route.reshape(1, cap_dev),
        caption_clip.reshape(1, cap_dev),
    )
    return loss.reshape(clip_dev), grad


def solution(mesh):
    in_specs = (
        P(("dp", "fsdp"), None, None),
        P(("dp", "fsdp"), None),
        P(),
        P(("dp", "fsdp"), None),
        P("fsdp", None),
        P(("dp", "fsdp"), None),
        P(("dp", "fsdp")),
    )
    out_specs = (P(("dp", "fsdp")), P(("dp", "fsdp"), None))
    return jax.shard_map(local, mesh=mesh, in_specs=in_specs, out_specs=out_specs, check_vma=False)
```

```python
import functools

import jax
import jax.numpy as jnp
from jax import lax
from jax.experimental import pallas as pl
from jax.experimental.pallas import tpu as pltpu
from jax.sharding import PartitionSpec as P

HALVES = 2
LANES = 128
F32 = jnp.float32
BF16 = jnp.bfloat16


def normalize(values):
    return values * lax.rsqrt(jnp.sum(values * values, axis=-1, keepdims=True) + 1e-06)


def gelu(x):
    return 0.5 * x * (1.0 + jnp.tanh(0.7978845608028654 * (x + 0.044715 * (x * x * x))))


def remote(src, dst, send, recv, target):
    return pltpu.make_async_remote_copy(
        src_ref=src,
        dst_ref=dst,
        send_sem=send,
        recv_sem=recv,
        device_id=target,
        device_id_type=pl.DeviceIdType.MESH,
    )


def kernel(
    groups,
    shards,
    frames_hbm,
    weight_hbm,
    caps_hbm,
    text_hbm,
    mask_ref,
    route_ref,
    clip_ref,
    grad_out,
    loss_out,
    frames_v,
    weight_v,
    own_caps,
    text_v,
    cap_recv,
    part_send,
    part_recv,
    clip_slots,
    grp_rows,
    all_motion,
    grad_send,
    grad_recv,
    loss_send,
    loss_recv,
    local_sem,
    cap_ss,
    cap_rs,
    part_ss,
    part_rs,
    m1_ss,
    m1_rs,
    m2_ss,
    m2_rs,
    g_ss,
    g_rs,
):
    me_g, me_f = lax.axis_index("dp"), lax.axis_index("fsdp")
    clip_dev, frame_count, _ = frames_v.shape
    cap_dev, depth = own_caps.shape
    emb = text_v.shape[1]
    rows = cap_dev // HALVES
    grp_clips = shards * clip_dev
    clips = groups * grp_clips
    devices = groups * shards
    me = me_g * shards + me_f

    def shard(k):
        return lax.rem(me_f + (k + shards), shards)

    def group(k):
        return lax.rem(me_g + (k + groups), groups)

    def columns(owner):
        return pl.ds(pl.multiple_of(owner * depth, depth), depth)

    loads = [
        pltpu.make_async_copy(frames_hbm, frames_v, local_sem.at[0]),
        pltpu.make_async_copy(weight_hbm, weight_v, local_sem.at[1]),
        pltpu.make_async_copy(text_hbm, text_v, local_sem.at[2]),
        pltpu.make_async_copy(caps_hbm.at[:, columns(me_f)], own_caps, local_sem.at[3]),
    ]
    for load in loads:
        load.start()

    barrier = pltpu.get_barrier_semaphore()
    for k in range(1, shards):
        pl.semaphore_signal(
            barrier, inc=1, device_id={"fsdp": shard(k)}, device_id_type=pl.DeviceIdType.MESH
        )
    for k in range(1, groups):
        pl.semaphore_signal(
            barrier, inc=1, device_id={"dp": group(k)}, device_id_type=pl.DeviceIdType.MESH
        )
    pl.semaphore_wait(barrier, shards + groups - 2)

    offsets = sorted(range(1, shards), key=lambda k: abs(k - shards // 2))
    cap_copies = {}

    def send_captions(h):
        for k in offsets:
            cap_copies[h, k] = remote(
                caps_hbm.at[pl.ds(h * rows, rows), columns(shard(k))],
                cap_recv.at[h, k - 1],
                cap_ss.at[h, k - 1],
                cap_rs.at[h, k - 1],
                {"fsdp": shard(k)},
            )
            cap_copies[h, k].start()

    send_captions(0)

    loads[0].wait()
    loads[1].wait()
    eye = (
        lax.broadcasted_iota(jnp.int32, (frame_count, frame_count), 0)
        == lax.broadcasted_iota(jnp.int32, (frame_count, frame_count), 1)
    ).astype(F32)
    for clip in range(clip_dev):
        hidden = gelu(jnp.dot(frames_v[clip], weight_v[...], preferred_element_type=F32))
        keep = jnp.sum(eye * mask_ref[pl.ds(clip, 1), :].astype(F32), axis=1, keepdims=True)
        pooled = jnp.sum(hidden * keep, axis=0, keepdims=True)
        clip_slots[me_f, pl.ds(clip, 1), :] = normalize(pooled).astype(BF16).astype(F32)
    m1 = []
    for k in range(1, shards):
        copy = remote(
            clip_slots.at[me_f],
            clip_slots.at[me_f],
            m1_ss.at[k - 1],
            m1_rs.at[k - 1],
            {"fsdp": shard(k)},
        )
        copy.start()
        m1.append(copy)

    for h in range(1, HALVES):
        send_captions(h)

    loads[2].wait()
    loads[3].wait()
    text_raw = jnp.dot(own_caps[...], text_v[...], preferred_element_type=F32)
    part_copies = []

    for k in range(1, shards):
        remote(
            clip_slots.at[me_f],
            clip_slots.at[shard(-k)],
            m1_ss.at[k - 1],
            m1_rs.at[k - 1],
            {"fsdp": shard(-k)},
        ).wait_recv()
    for f in range(shards):
        grp_rows[pl.ds(f * clip_dev, clip_dev), :] = clip_slots[f]
    all_motion[me_g] = grp_rows[...].astype(BF16)
    m2 = []
    for k in range(1, groups):
        copy = remote(
            all_motion.at[me_g],
            all_motion.at[me_g],
            m2_ss.at[k - 1],
            m2_rs.at[k - 1],
            {"dp": group(k)},
        )
        copy.start()
        m2.append(copy)

    def project(h):
        for k in offsets:
            cap_copies[h, k].wait_recv()
        arrived = cap_recv[h].reshape((shards - 1) * rows, depth)
        partial = jnp.dot(arrived, text_v[...], preferred_element_type=F32).astype(BF16)
        for k in offsets:
            part_send[h, k - 1] = partial[(k - 1) * rows : k * rows, :]
            copy = remote(
                part_send.at[h, k - 1],
                part_recv.at[k - 1, pl.ds(h * rows, rows)],
                part_ss.at[h, k - 1],
                part_rs.at[h, k - 1],
                {"fsdp": shard(-k)},
            )
            copy.start()
            part_copies.append(copy)

    for h in range(HALVES):
        project(h)

    for k in range(1, groups):
        remote(
            all_motion.at[me_g],
            all_motion.at[group(-k)],
            m2_ss.at[k - 1],
            m2_rs.at[k - 1],
            {"dp": group(-k)},
        ).wait_recv()
    motion = all_motion[...].reshape(clips, emb)

    route, chosen = route_ref[...], clip_ref[...]
    r = lax.broadcasted_iota(jnp.int32, (clips, cap_dev), 0)
    in_group = (r // grp_clips) == route
    target = r == route * grp_clips + chosen

    for copy in part_copies:
        copy.wait_recv()
    for k in range(1, shards):
        text_raw = text_raw + part_recv[k - 1].astype(F32)
    text_emb = normalize(text_raw).astype(BF16)

    scores = (
        lax.dot_general(motion, text_emb, (((1,), (1,)), ((), ())), preferred_element_type=F32)
        / 0.07
    )
    power = jnp.where(in_group, jnp.exp(scores), 0.0)
    total = jnp.sum(power, axis=0, keepdims=True)
    lse = jnp.log(total)
    onehot = target.astype(F32)
    losses = lse - jnp.sum(onehot * scores, axis=0, keepdims=True)
    coefficient = (power * (1.0 / total) - onehot).astype(BF16)
    grad = jnp.dot(coefficient, text_emb, preferred_element_type=F32)
    loss_term = jnp.sum(onehot * losses, axis=1, keepdims=True)
    lane = lax.broadcasted_iota(jnp.int32, (clips, LANES), 1)
    row = lax.broadcasted_iota(jnp.int32, (clips, LANES), 0)
    spread = jnp.where(lane == (row & (clip_dev - 1)), loss_term, 0.0)
    owner = (
        lax.broadcasted_iota(jnp.int32, (devices, clips), 1) // clip_dev
        == lax.broadcasted_iota(jnp.int32, (devices, clips), 0)
    )
    owner = owner.astype(F32).astype(BF16)
    high = spread.astype(BF16)
    low = (spread - high.astype(F32)).astype(BF16)
    loss_rows = jnp.dot(owner, high, preferred_element_type=F32) + jnp.dot(
        owner, low, preferred_element_type=F32
    )
    loss_send[...] = loss_rows.reshape(devices, 1, LANES)
    grad = grad.reshape(devices // 2, 2 * clip_dev, emb)
    upper = lax.broadcasted_iota(jnp.int32, (devices // 2, 2 * clip_dev, LANES), 1) < clip_dev
    even, odd = [], []
    for c in range(0, emb // LANES, 2):
        one = grad[:, :, c * LANES : (c + 1) * LANES]
        two = grad[:, :, (c + 1) * LANES : (c + 2) * LANES]
        even.append(jnp.where(upper, one, pltpu.roll(two, clip_dev, axis=1)))
        odd.append(jnp.where(upper, pltpu.roll(one, clip_dev, axis=1), two))
    grad_send[:, 0] = jnp.concatenate(even, axis=1).astype(BF16)
    grad_send[:, 1] = jnp.concatenate(odd, axis=1).astype(BF16)

    def to_owner(step, carry):
        k = step
        to = lax.rem(me + k, devices)
        where = {"dp": to // shards, "fsdp": lax.rem(to, shards)}
        remote(
            grad_send.at[to // 2, lax.rem(to, 2)], grad_recv.at[k - 1], g_ss.at[0], g_rs.at[0], where
        ).start()
        remote(loss_send.at[to], loss_recv.at[k - 1], g_ss.at[1], g_rs.at[1], where).start()
        return carry

    lax.fori_loop(1, devices, to_owner, 0)
    where = {"dp": me_g, "fsdp": shard(1)}
    grad_all = remote(grad_recv, grad_recv, g_ss.at[0], g_rs.at[0], where)
    loss_all = remote(loss_recv, loss_recv, g_ss.at[1], g_rs.at[1], where)
    grad_all.wait_recv()
    final = grad_send[me // 2, lax.rem(me, 2)].astype(F32)
    final = (final + jnp.sum(grad_recv[...].astype(F32), axis=0)) / 0.07
    for c in range(emb // LANES):
        grad_out[:, pl.ds(c * LANES, LANES)] = final[c * clip_dev : (c + 1) * clip_dev, :]
    loss_all.wait_recv()
    loss = loss_send[me] + jnp.sum(loss_recv[...], axis=0)
    loss_out[...] = loss * (clip_dev / cap_dev)

    grad_all.wait_send()
    loss_all.wait_send()
    for copy in [*cap_copies.values(), *part_copies, *m1, *m2]:
        copy.wait_send()


def local(
    frames, frame_mask, motion_weight, caption_feats, text_weight, caption_route, caption_clip
):
    groups, shards = lax.axis_size("dp"), lax.axis_size("fsdp")
    clip_dev = frames.shape[0]
    cap_dev = caption_feats.shape[0]
    depth, emb = text_weight.shape
    rows = cap_dev // HALVES
    devices = groups * shards
    sub = clip_dev * emb // LANES
    limit = (56 if devices <= 64 else 56) * 1024 * 1024
    hbm, vmem = pl.BlockSpec(memory_space=pltpu.HBM), pl.BlockSpec(memory_space=pltpu.VMEM)
    dma = pltpu.SemaphoreType.DMA
    grad, loss = pl.pallas_call(
        functools.partial(kernel, groups, shards),
        out_shape=(
            jax.ShapeDtypeStruct((clip_dev, emb), F32),
            jax.ShapeDtypeStruct((1, LANES), F32),
        ),
        in_specs=[hbm] * 4 + [vmem] * 3,
        out_specs=(vmem, vmem),
        scratch_shapes=[
            pltpu.VMEM(frames.shape, BF16),
            pltpu.VMEM(motion_weight.shape, BF16),
            pltpu.VMEM((cap_dev, depth), BF16),
            pltpu.VMEM((depth, emb), BF16),
            pltpu.VMEM((HALVES, shards - 1, rows, depth), BF16),
            pltpu.VMEM((HALVES, shards - 1, rows, emb), BF16),
            pltpu.VMEM((shards - 1, cap_dev, emb), BF16),
            pltpu.VMEM((shards, clip_dev, emb), F32),
            pltpu.VMEM((shards * clip_dev, emb), F32),
            pltpu.VMEM((groups, shards * clip_dev, emb), BF16),
            pltpu.VMEM((devices // 2, 2, sub, LANES), BF16),
            pltpu.VMEM((devices - 1, sub, LANES), BF16),
            pltpu.VMEM((devices, 1, LANES), F32),
            pltpu.VMEM((devices - 1, 1, LANES), F32),
            dma((4,)),
            dma((HALVES, shards - 1)),
            dma((HALVES, shards - 1)),
            dma((HALVES, shards - 1)),
            dma((HALVES, shards - 1)),
            dma((shards - 1,)),
            dma((shards - 1,)),
            dma((groups - 1,)),
            dma((groups - 1,)),
            dma((2,)),
            dma((2,)),
        ],
        compiler_params=pltpu.CompilerParams(
            collective_id=0, has_side_effects=True, vmem_limit_bytes=limit
        ),
    )(
        frames,
        motion_weight,
        caption_feats,
        text_weight,
        frame_mask,
        caption_route.reshape(1, cap_dev),
        caption_clip.reshape(1, cap_dev),
    )
    return loss[0, :clip_dev], grad


def solution(mesh):
    in_specs = (
        P(("dp", "fsdp"), None, None),
        P(("dp", "fsdp"), None),
        P(),
        P(("dp", "fsdp"), None),
        P("fsdp", None),
        P(("dp", "fsdp"), None),
        P(("dp", "fsdp")),
    )
    out_specs = (P(("dp", "fsdp")), P(("dp", "fsdp"), None))
    return jax.shard_map(local, mesh=mesh, in_specs=in_specs, out_specs=out_specs, check_vma=False)
```
